32 devices in a mesh: strip: 4 (over x, core), section: 8 (over z, y).
Axes of the slice: x: 2, y: 2, z: 4, core: 2. Of those that a mesh axis runs over, the one named last changes fastest.
Arguments:
- features: bfloat16 [8, 8, 128, 1024], P(None, 'strip'), may hold values from -6 to 6
- tile_list: int32 [8, 4, 16], P(None, 'strip'), may hold values from 0 to 15, as said below
- w_reduce: bfloat16 [8, 1024, 256], P('section'), may hold values from -0.1875 to 0.1875
- bias_reduce: bfloat16 [8, 256], P('section'), may hold values from -3 to 3
- w_spatial: bfloat16 [8, 3, 3, 256, 256], P('section'), may hold values from -0.125 to 0.125
- bias_spatial: bfloat16 [8, 256], P('section'), may hold values from -3 to 3
- w_expand: bfloat16 [8, 256, 1024], P('section'), may hold values from -0.375 to 0.375
- bias_expand: bfloat16 [8, 1024], P('section'), may hold values from -3 to 3
Outputs:
- block_maps: bfloat16 [8, 8, 8, 128, 1024], P('section', None, 'strip')
The draws below stay inside these ranges and needn't reach their ends.
Inputs may be any that keep to these rules, and one draw needn't show every extreme that they name: `tile_list`: each strip's row lists the tissue tiles of that strip, padded to 16 entries by repeats of its first entry; in each slide window one strip is all tissue.
All inputs are finite; a program needn't handle non-finite values.
Results may differ from the reference program's by a relative error of at most 0.02.
Values may be sent and summed in bfloat16 or wider, within the bound.
A program may use at most 64 MiB of HBM per device.

```python
import jax
import jax.numpy as jnp

C = 1024
BOT = 256
SLIDES = 8
R = 2
TILES = 16
TILE_W = 8
W = 128
STRIPS = 4
H = 8
SEGMENTS = 8


def draw_tile_list(key, part):
    key_perm, key_count, key_full = jax.random.split(key, 3)
    keys = jax.random.split(key_perm, SLIDES * STRIPS)
    orders = jax.vmap(lambda one_key: jax.random.permutation(one_key, TILES))(keys).reshape(SLIDES, STRIPS, TILES)
    counts = jax.random.randint(key_count, (SLIDES, STRIPS), 1, TILES + 1)
    full_strip = jax.random.randint(key_full, (SLIDES,), 0, STRIPS)
    counts = jnp.where(jnp.arange(STRIPS)[None, :] == full_strip[:, None], TILES, counts)
    position = jnp.arange(TILES)[None, None, :]
    listed = jnp.where(position < counts[..., None], orders, orders[..., :1])
    return listed.astype(jnp.int32)


def shard_levels(own_key, dims, shards, smallest, largest):
    level, own = 1.0, jax.random.fold_in(own_key, 6)
    for dim, blocks in shards:
        steps = jnp.exp(jax.random.uniform(jax.random.fold_in(own, dim), (blocks,), jnp.float32, smallest / len(shards), largest / len(shards)))
        level = level * jnp.repeat(steps, dims[dim] // blocks).reshape([-1 if axis == dim else 1 for axis in range(len(dims))])
    return level


def centred(rng, extent, width, limit, cuts=(), kind=jnp.bfloat16):
    drawn = width * jax.random.normal(rng, extent, jnp.float32)
    if cuts:
        drawn = drawn * shard_levels(rng, extent, cuts, -0.22, 0.18)
    return jnp.clip(drawn, -limit, limit).astype(kind)


def setup_inputs(seed: int = 0) -> dict:
    streams_of = jax.random.split(jax.random.key(seed), 9)
    features = centred(streams_of[0], (SLIDES, H, W, C), 1.0, 6.0, ((1, 4),))
    tile_list = draw_tile_list(jax.random.fold_in(streams_of[8], 71), 0)
    w_reduce = centred(streams_of[2], (SEGMENTS, C, BOT), C ** -0.5, 0.1875, ((0, 8),))
    bias_reduce = centred(streams_of[3], (SEGMENTS, BOT), 0.5, 3.0, ((0, 8),))
    w_spatial = centred(streams_of[4], (SEGMENTS, 3, 3, BOT, BOT), (9 * BOT) ** -0.5, 0.125, ((0, 8),))
    bias_spatial = centred(streams_of[5], (SEGMENTS, BOT), 0.5, 3.0, ((0, 8),))
    w_expand = centred(streams_of[6], (SEGMENTS, BOT, C), BOT ** -0.5, 0.375, ((0, 8),))
    bias_expand = centred(streams_of[7], (SEGMENTS, C), 0.5, 3.0, ((0, 8),))
    return {"features": features, "tile_list": tile_list, "w_reduce": w_reduce, "bias_reduce": bias_reduce, "w_spatial": w_spatial, "bias_spatial": bias_spatial, "w_expand": w_expand, "bias_expand": bias_expand}


def tissue_mask(tile_list):
    columns = jnp.arange(TILES, dtype=jnp.int32)
    hits = jnp.any(tile_list[..., :, None] == columns[None, None, None, :], axis=-2)
    tissue = hits.astype(jnp.float32)
    tissue = jnp.repeat(tissue, R, axis=1)
    return jnp.repeat(tissue, TILE_W, axis=2)


def block_ref(maps, tissue, w_one, b_one, w_two, b_two, w_three, b_three):
    rows, cols, chans = maps.shape
    flat = maps.reshape(-1, chans)
    reduced = jax.nn.relu(jnp.dot(flat, w_one, preferred_element_type=jnp.float32) + b_one.astype(jnp.float32))
    reduced = reduced.astype(jnp.bfloat16).reshape(rows, cols, BOT)
    padded = jnp.pad(reduced, ((1, 1), (1, 1), (0, 0)))
    accumulated = jnp.zeros((rows * cols, BOT), jnp.float32)
    for row_off in range(3):
        for col_off in range(3):
            window = padded[row_off:row_off + rows, col_off:col_off + cols].reshape(-1, BOT)
            accumulated = accumulated + jnp.dot(window, w_two[row_off, col_off], preferred_element_type=jnp.float32)
    spatial = jax.nn.relu(accumulated + b_two.astype(jnp.float32)).astype(jnp.bfloat16)
    expanded = jnp.dot(spatial, w_three, preferred_element_type=jnp.float32) + b_three.astype(jnp.float32)
    result = jax.nn.relu(flat.astype(jnp.float32) + expanded) * tissue.reshape(-1, 1)
    return result.astype(jnp.bfloat16).reshape(rows, cols, chans)


def reference(features, tile_list, w_reduce, bias_reduce, w_spatial, bias_spatial, w_expand, bias_expand):
    tissue = tissue_mask(tile_list)
    per_block = []
    maps = [features[slide_index] for slide_index in range(SLIDES)]
    for block_index in range(SEGMENTS):
        maps = [block_ref(maps[slide_index], tissue[slide_index], w_reduce[block_index], bias_reduce[block_index],
                          w_spatial[block_index], bias_spatial[block_index], w_expand[block_index],
                          bias_expand[block_index]) for slide_index in range(SLIDES)]
        per_block.append(jnp.stack(maps, 0))
    return jnp.stack(per_block, 0)
```

```python
import functools

import jax
import jax.numpy as jnp
from jax import lax
from jax.experimental import pallas as pl
from jax.experimental.pallas import tpu as pltpu
from jax.sharding import PartitionSpec as P

TILE_W = 8
F32 = jnp.float32
BF16 = jnp.bfloat16


def tissue_mask(tile_list, rows):
    tiles_count = tile_list.shape[-1]
    columns = jnp.arange(tiles_count, dtype=jnp.int32)
    hits = jnp.any(tile_list[..., :, None] == columns[None, None, None, :], axis=-2)
    tissue = hits.astype(jnp.float32)
    tissue = jnp.repeat(tissue, rows, axis=1)
    return jnp.repeat(tissue, TILE_W, axis=2)


def kernel(
    strips, sections, half, cols, chans, inner,
    feat, mask, w1, w2, w3, bias, out,
    inbuf, mid, fin, stage, halo, v1, v2, v3, vb,
    feat_sem, own_sem, in_sem, fwd_sem, loc_sem, out_send, out_recv,
    halo_send, halo_recv, w_send, w_recv, m_send, m_recv,
):
    p = lax.axis_index("strip")
    s = lax.axis_index("section")
    pair = s // 2
    b = s % 2
    c = p % 2
    pairs = sections // 2
    partner = {"section": s + 1 - 2 * b}
    mate = {"strip": p + 1 - 2 * c}
    up, down = {"strip": p - 1}, {"strip": p + 1}
    ahead, behind = {"section": s + 2}, {"section": s - 2}
    has_up, has_down = p > 0, p < strips - 1
    first, last = pair == 0, pair == pairs - 1
    MESH = pl.DeviceIdType.MESH

    def remote(src, dst, send, recv, to):
        return pltpu.make_async_remote_copy(
            src_ref=src, dst_ref=dst, send_sem=send, recv_sem=recv, device_id=to, device_id_type=MESH
        )

    barrier = pltpu.get_barrier_semaphore()

    def greet(to):
        pl.semaphore_signal(barrier, inc=1, device_id=to, device_id_type=MESH)

    greet(partner)
    pl.when(has_up)(lambda: greet(up))
    pl.when(has_down)(lambda: greet(down))
    pl.when(jnp.logical_not(last))(lambda: greet(ahead))
    pl.when(jnp.logical_not(first))(lambda: greet(behind))

    weights = ((w1, v1), (w2, v2), (w3, v3))

    def own_copies():
        made = [pltpu.make_async_copy(w, v.at[b], own_sem.at[i]) for i, (w, v) in enumerate(weights)]
        return made + [pltpu.make_async_copy(bias, vb.at[b], own_sem.at[3])]

    def feat_copy(j):
        return pltpu.make_async_copy(feat.at[b * half + j], inbuf.at[j], feat_sem.at[j])

    for one in own_copies():
        one.start()

    @pl.when(first)
    def _():
        for j in range(half):
            feat_copy(j).start()

    def zero_edge(side):
        def body(t, carry):
            halo[t, side] = jnp.zeros((cols, inner), BF16)
            return carry

        lax.fori_loop(0, 2 * half, body, 0)

    pl.when(jnp.logical_not(has_up))(lambda: zero_edge(0))
    pl.when(jnp.logical_not(has_down))(lambda: zero_edge(1))

    peers = 1 + sum(jnp.where(met, 1, 0) for met in (has_up, has_down, pair < pairs - 1, pair > 0))
    pl.semaphore_wait(barrier, peers)

    def part_copies():
        made = []
        for i, (w, v) in enumerate(weights):
            depth = w.shape[0] // 2
            rows = pl.ds(pl.multiple_of(c * depth, depth), depth)
            made.append(remote(w.at[rows], v.at[b, rows], w_send.at[i], w_recv.at[i], partner))
        made.append(remote(bias, vb.at[b], w_send.at[3], w_recv.at[3], partner))
        return made

    def mate_copies():
        made = []
        for i, (w, v) in enumerate(weights):
            depth = w.shape[0] // 2
            rows = pl.ds(pl.multiple_of(c * depth, depth), depth)
            where = v.at[1 - b, rows]
            made.append(remote(where, where, m_send.at[i], m_recv.at[i], mate))
        return made

    for i in (3, 0, 1, 2):
        part_copies()[i].start()

    def wait_own():
        for one in own_copies():
            one.wait()

    def wait_other():
        part_copies()[3].wait_recv()
        for i in range(3):
            part_copies()[i].wait_recv()
            mate_copies()[i].start()
        for i in range(3):
            mate_copies()[i].wait_recv()

    def halo_up(t):
        return remote(
            stage.at[t, pl.ds(0, cols)], halo.at[t, 1], halo_send.at[t, 0], halo_recv.at[t, 1], up
        )

    def halo_down(t):
        return remote(
            stage.at[t, pl.ds(cols, cols)], halo.at[t, 0], halo_send.at[t, 1], halo_recv.at[t, 0], down
        )

    column = lax.broadcasted_iota(jnp.int32, (2 * cols, inner), 0) % cols

    def dot(lhs, rhs):
        return jnp.dot(lhs, rhs, preferred_element_type=F32)

    def block(which, j, src, dst):
        t = which * half + j
        reduced = dot(src[j], v1[which]) + vb[which, 0:1, 0:inner]
        stage[t] = jnp.maximum(reduced, 0.0).astype(BF16)
        pl.when(has_up)(lambda: halo_up(t).start())
        pl.when(has_down)(lambda: halo_down(t).start())

        def tap(dy, dx):
            return v2[which, pl.ds((dy * 3 + dx) * inner, inner), :]

        both = stage[t]
        upper, lower = both[:cols], both[cols:]
        sums = []
        for dx in range(3):
            centre = dot(both, tap(1, dx))
            cross = jnp.concatenate([dot(lower, tap(2, dx)), dot(upper, tap(0, dx))], axis=0)
            sums.append(centre + cross)
        pl.when(has_up)(lambda: halo_down(t).wait_recv())
        pl.when(has_down)(lambda: halo_up(t).wait_recv())
        above, below = halo[t, 0], halo[t, 1]
        for dx in range(3):
            sums[dx] += jnp.concatenate([dot(above, tap(0, dx)), dot(below, tap(2, dx))], axis=0)
        left = jnp.where(column == 0, 0.0, pltpu.roll(sums[0], 1, 0))
        right = jnp.where(column == cols - 1, 0.0, pltpu.roll(sums[2], 2 * cols - 1, 0))
        total = sums[1] + left + right + vb[which, 1:2, 0:inner]
        spatial = jnp.maximum(total, 0.0).astype(BF16)
        kept = mask[b * half + j][:, 0:1]
        for low in range(0, chans, inner):
            span = pl.ds(low, inner)
            value = src[j, :, span].astype(F32) + dot(spatial, v3[which, :, span]) + vb[which, 2:3, span]
            dst[j, :, span] = (jnp.maximum(value, 0.0) * kept).astype(BF16)

    def in_copy(j):
        return remote(fin.at[j], inbuf.at[j], fwd_sem.at[j], in_sem.at[j], ahead)

    def out_local(buffer, j):
        return pltpu.make_async_copy(buffer.at[j], out.at[b * half + j], loc_sem.at[j])

    def out_remote(buffer, j):
        return remote(buffer.at[j], out.at[b * half + j], out_send.at[j], out_recv.at[j], partner)

    pl.when(b == 0)(wait_own)
    pl.when(b == 1)(wait_other)

    def one_slide(j, carry):
        pl.when(first)(lambda: feat_copy(j).wait())
        pl.when(jnp.logical_not(first))(lambda: in_copy(j).wait_recv())
        block(0, j, inbuf, mid)
        pl.when(b == 0)(lambda: out_local(mid, j).start())
        pl.when(b == 1)(lambda: out_remote(mid, j).start())

        @pl.when(j == 0)
        def _():
            pl.when(b == 0)(wait_other)
            pl.when(b == 1)(wait_own)

        block(1, j, mid, fin)
        pl.when(jnp.logical_not(last))(lambda: in_copy(j).start())
        pl.when(b == 1)(lambda: out_local(fin, j).start())
        pl.when(b == 0)(lambda: out_remote(fin, j).start())
        return carry

    lax.fori_loop(0, half, one_slide, 0)

    for one in part_copies() + mate_copies():
        one.wait_send()

    def drain(j, carry):
        for t in (j, half + j):
            pl.when(has_up)(lambda t=t: halo_up(t).wait_send())
            pl.when(has_down)(lambda t=t: halo_down(t).wait_send())
        pl.when(jnp.logical_not(last))(lambda: in_copy(j).wait_send())
        out_local(mid, j).wait()
        out_remote(mid, j).wait()
        return carry

    lax.fori_loop(0, half, drain, 0)


def shards(
    strips, sections,
    features, tile_list, w_reduce, bias_reduce, w_spatial, bias_spatial, w_expand, bias_expand,
):
    slides, rows, cols, chans = features.shape
    inner = w_reduce.shape[-1]
    half = slides // 2
    cells = rows * cols
    tissue = tissue_mask(tile_list, rows).reshape(slides, cells, 1)
    mask = jnp.broadcast_to(tissue, (slides, cells, 128))
    bias = jnp.zeros((8, chans), F32)
    bias = bias.at[0, :inner].set(bias_reduce[0].astype(F32))
    bias = bias.at[1, :inner].set(bias_spatial[0].astype(F32))
    bias = bias.at[2].set(bias_expand[0].astype(F32))
    dma = pltpu.SemaphoreType.DMA
    anywhere = pl.BlockSpec(memory_space=pl.ANY)
    result = pl.pallas_call(
        functools.partial(kernel, strips, sections, half, cols, chans, inner),
        out_shape=jax.ShapeDtypeStruct((slides, cells, chans), BF16),
        in_specs=[anywhere, pl.BlockSpec(memory_space=pltpu.VMEM)] + [anywhere] * 4,
        out_specs=anywhere,
        scratch_shapes=[
            pltpu.VMEM((half, cells, chans), BF16),
            pltpu.VMEM((half, cells, chans), BF16),
            pltpu.VMEM((half, cells, chans), BF16),
            pltpu.VMEM((2 * half, cells, inner), BF16),
            pltpu.VMEM((2 * half, 2, cols, inner), BF16),
            pltpu.VMEM((2, chans, inner), BF16),
            pltpu.VMEM((2, 9 * inner, inner), BF16),
            pltpu.VMEM((2, inner, chans), BF16),
            pltpu.VMEM((2, 8, chans), F32),
            dma((half,)), dma((4,)), dma((half,)), dma((half,)), dma((half,)), dma((half,)), dma((half,)),
            dma((2 * half, 2)), dma((2 * half, 2)), dma((4,)), dma((4,)), dma((3,)), dma((3,)),
        ],
        compiler_params=pltpu.CompilerParams(
            collective_id=0, has_side_effects=True, vmem_limit_bytes=40 * 1024 * 1024
        ),
    )(
        features.reshape(slides, cells, chans),
        mask,
        w_reduce[0],
        w_spatial.reshape(9 * inner, inner),
        w_expand[0],
        bias,
    )
    return result.reshape(1, slides, rows, cols, chans)


def solution(mesh):
    in_specs = (
        P(None, "strip", None, None),
        P(None, "strip", None),
        P("section", None, None),
        P("section", None),
        P("section", None, None, None, None),
        P("section", None),
        P("section", None, None),
        P("section", None),
    )
    out_specs = P("section", None, "strip", None, None)
    body = functools.partial(shards, mesh.shape["strip"], mesh.shape["section"])
    return jax.shard_map(body, mesh=mesh, in_specs=in_specs, out_specs=out_specs, check_vma=False)
```

```python
import functools

import jax
import jax.numpy as jnp
from jax import lax
from jax.experimental import pallas as pl
from jax.experimental.pallas import tpu as pltpu
from jax.sharding import PartitionSpec as P

TILE_W = 8
F32 = jnp.float32
BF16 = jnp.bfloat16


def tissue_mask(tile_list, rows):
    tiles_count = tile_list.shape[-1]
    columns = jnp.arange(tiles_count, dtype=jnp.int32)
    hits = jnp.any(tile_list[..., :, None] == columns[None, None, None, :], axis=-2)
    tissue = hits.astype(jnp.float32)
    tissue = jnp.repeat(tissue, rows, axis=1)
    return jnp.repeat(tissue, TILE_W, axis=2)


def kernel(
    strips, sections, half, cols, chans, inner,
    feat, mask, w1, w2, w3, bias, out,
    inbuf, mid, fin, stage, halo, v1, v2, v3, vb,
    feat_sem, own_sem, in_sem, fwd_sem, loc_sem, out_send, out_recv,
    halo_send, halo_recv, w_send, w_recv, m_send, m_recv,
):
    p = lax.axis_index("strip")
    s = lax.axis_index("section")
    pair = s // 2
    b = s % 2
    c = p % 2
    q = p % 4
    side = q // 2
    pairs = sections // 2
    partner = {"section": s + 1 - 2 * b}
    mate = {"strip": p + 1 - 2 * c}
    across = {"strip": p + 2 - 4 * side}
    up, down = {"strip": p - 1}, {"strip": p + 1}
    ahead, behind = {"section": s + 2}, {"section": s - 2}
    has_up, has_down = p > 0, p < strips - 1
    first, last = pair == 0, pair == pairs - 1
    MESH = pl.DeviceIdType.MESH

    def remote(src, dst, send, recv, to):
        return pltpu.make_async_remote_copy(
            src_ref=src, dst_ref=dst, send_sem=send, recv_sem=recv, device_id=to, device_id_type=MESH
        )

    barrier = pltpu.get_barrier_semaphore()

    def greet(to):
        pl.semaphore_signal(barrier, inc=1, device_id=to, device_id_type=MESH)

    greet(partner)
    greet(across)
    pl.when(has_up)(lambda: greet(up))
    pl.when(has_down)(lambda: greet(down))
    pl.when(jnp.logical_not(last))(lambda: greet(ahead))
    pl.when(jnp.logical_not(first))(lambda: greet(behind))

    weights = ((w1, v1), (w2, v2), (w3, v3))

    def own_copies():
        made = [pltpu.make_async_copy(w, v.at[b], own_sem.at[i]) for i, (w, v) in enumerate(weights)]
        return made + [pltpu.make_async_copy(bias, vb.at[b], own_sem.at[3])]

    def feat_copy(j):
        return pltpu.make_async_copy(feat.at[b * half + j], inbuf.at[j], feat_sem.at[j])

    for one in own_copies():
        one.start()

    @pl.when(first)
    def _():
        for j in range(half):
            feat_copy(j).start()

    def zero_edge(edge):
        def body(t, carry):
            halo[t, edge] = jnp.zeros((cols, inner), BF16)
            return carry

        lax.fori_loop(0, 2 * half, body, 0)

    pl.when(jnp.logical_not(has_up))(lambda: zero_edge(0))
    pl.when(jnp.logical_not(has_down))(lambda: zero_edge(1))

    peers = 2 + sum(jnp.where(met, 1, 0) for met in (has_up, has_down, pair < pairs - 1, pair > 0))
    pl.semaphore_wait(barrier, peers)

    def quarter(i, which):
        depth = weights[i][0].shape[0] // 4
        return pl.ds(pl.multiple_of(which * depth, depth), depth)

    def part_copy(i):
        if i == 3:
            return remote(bias, vb.at[b], w_send.at[3], w_recv.at[3], partner)
        w, v = weights[i]
        rows = quarter(i, q)
        return remote(w.at[rows], v.at[b, rows], w_send.at[i], w_recv.at[i], partner)

    def spread(i, which, slot, to):
        where = weights[i][1].at[1 - b, quarter(i, which)]
        return remote(where, where, m_send.at[slot, i], m_recv.at[slot, i], to)

    def mate_copy(i):
        return spread(i, q, 0, mate)

    def across_copy(i):
        return spread(i, q, 1, across)

    def onward_copy(i):
        return spread(i, (q + 2) % 4, 2, mate)

    for i in (3, 0, 1, 2):
        part_copy(i).start()

    def wait_own():
        for one in own_copies():
            one.wait()

    def wait_other():
        part_copy(3).wait_recv()
        part_copy(0).wait_recv()
        across_copy(0).start()
        mate_copy(0).start()
        for i in range(3):
            if i < 2:
                part_copy(i + 1).wait_recv()
                across_copy(i + 1).start()
                mate_copy(i + 1).start()
            across_copy(i).wait_recv()
            onward_copy(i).start()
        for i in range(3):
            mate_copy(i).wait_recv()
            onward_copy(i).wait_recv()

    def halo_up(t):
        return remote(
            stage.at[t, pl.ds(0, cols)], halo.at[t, 1], halo_send.at[t, 0], halo_recv.at[t, 1], up
        )

    def halo_down(t):
        return remote(
            stage.at[t, pl.ds(cols, cols)], halo.at[t, 0], halo_send.at[t, 1], halo_recv.at[t, 0], down
        )

    column = lax.broadcasted_iota(jnp.int32, (2 * cols, inner), 0) % cols

    def dot(lhs, rhs):
        return jnp.dot(lhs, rhs, preferred_element_type=F32)

    def block(which, j, src, dst, arrived, finished):
        t = which * half + j
        for r in range(2):
            arrived(r)
            reduced = dot(src[j, pl.ds(r * cols, cols)], v1[which]) + vb[which, 0:1, 0:inner]
            stage[t, pl.ds(r * cols, cols)] = jnp.maximum(reduced, 0.0).astype(BF16)
            if r == 0:
                pl.when(has_up)(lambda: halo_up(t).start())
            else:
                pl.when(has_down)(lambda: halo_down(t).start())

        def tap(dy, dx):
            return v2[which, pl.ds((dy * 3 + dx) * inner, inner), :]

        both = stage[t]
        upper, lower = both[:cols], both[cols:]
        sums = []
        for dx in range(3):
            centre = dot(both, tap(1, dx))
            cross = jnp.concatenate([dot(lower, tap(2, dx)), dot(upper, tap(0, dx))], axis=0)
            sums.append(centre + cross)
        pl.when(has_up)(lambda: halo_down(t).wait_recv())
        pl.when(has_down)(lambda: halo_up(t).wait_recv())
        above, below = halo[t, 0], halo[t, 1]
        for dx in range(3):
            sums[dx] += jnp.concatenate([dot(above, tap(0, dx)), dot(below, tap(2, dx))], axis=0)
        left = jnp.where(column == 0, 0.0, pltpu.roll(sums[0], 1, 0))
        right = jnp.where(column == cols - 1, 0.0, pltpu.roll(sums[2], 2 * cols - 1, 0))
        total = sums[1] + left + right + vb[which, 1:2, 0:inner]
        spatial = jnp.maximum(total, 0.0).astype(BF16)
        for r in range(2):
            part = pl.ds(r * cols, cols)
            kept = mask[b * half + j, part, 0:1]
            for low in range(0, chans, inner):
                span = pl.ds(low, inner)
                value = dot(spatial[r * cols : (r + 1) * cols], v3[which, :, span])
                value += src[j, part, span].astype(F32) + vb[which, 2:3, span]
                dst[j, part, span] = (jnp.maximum(value, 0.0) * kept).astype(BF16)
            finished(r)

    def in_copy(j, r):
        part = pl.ds(r * cols, cols)
        return remote(
            fin.at[j, part], inbuf.at[j, part], fwd_sem.at[j, r], in_sem.at[j, r], ahead
        )

    def out_local(buffer, j):
        return pltpu.make_async_copy(buffer.at[j], out.at[b * half + j], loc_sem.at[j])

    def out_remote(buffer, j):
        return remote(buffer.at[j], out.at[b * half + j], out_send.at[j], out_recv.at[j], partner)

    pl.when(b == 0)(wait_own)
    pl.when(b == 1)(wait_other)

    def one_slide(j, carry):
        pl.when(first)(lambda: feat_copy(j).wait())

        def arrived(r):
            pl.when(jnp.logical_not(first))(lambda: in_copy(j, r).wait_recv())

        def finished(r):
            pl.when(jnp.logical_not(last))(lambda: in_copy(j, r).start())

        def nothing(r):
            pass

        block(0, j, inbuf, mid, arrived, nothing)
        pl.when(b == 0)(lambda: out_local(mid, j).start())
        pl.when(b == 1)(lambda: out_remote(mid, j).start())

        @pl.when(j == 0)
        def _():
            pl.when(b == 0)(wait_other)
            pl.when(b == 1)(wait_own)

        block(1, j, mid, fin, nothing, finished)
        pl.when(b == 1)(lambda: out_local(fin, j).start())
        pl.when(b == 0)(lambda: out_remote(fin, j).start())
        return carry

    lax.fori_loop(0, half, one_slide, 0)

    part_copy(3).wait_send()
    for i in range(3):
        part_copy(i).wait_send()
        mate_copy(i).wait_send()
        across_copy(i).wait_send()
        onward_copy(i).wait_send()

    def drain(j, carry):
        for t in (j, half + j):
            pl.when(has_up)(lambda t=t: halo_up(t).wait_send())
            pl.when(has_down)(lambda t=t: halo_down(t).wait_send())
        for r in range(2):
            pl.when(jnp.logical_not(last))(lambda r=r: in_copy(j, r).wait_send())
        out_local(mid, j).wait()
        out_remote(mid, j).wait()
        return carry

    lax.fori_loop(0, half, drain, 0)


def shards(
    strips, sections,
    features, tile_list, w_reduce, bias_reduce, w_spatial, bias_spatial, w_expand, bias_expand,
):
    slides, rows, cols, chans = features.shape
    inner = w_reduce.shape[-1]
    half = slides // 2
    cells = rows * cols
    tissue = tissue_mask(tile_list, rows).reshape(slides, cells, 1)
    mask = jnp.broadcast_to(tissue, (slides, cells, 128))
    bias = jnp.zeros((8, chans), F32)
    bias = bias.at[0, :inner].set(bias_reduce[0].astype(F32))
    bias = bias.at[1, :inner].set(bias_spatial[0].astype(F32))
    bias = bias.at[2].set(bias_expand[0].astype(F32))
    dma = pltpu.SemaphoreType.DMA
    anywhere = pl.BlockSpec(memory_space=pl.ANY)
    result = pl.pallas_call(
        functools.partial(kernel, strips, sections, half, cols, chans, inner),
        out_shape=jax.ShapeDtypeStruct((slides, cells, chans), BF16),
        in_specs=[anywhere, pl.BlockSpec(memory_space=pltpu.VMEM)] + [anywhere] * 4,
        out_specs=anywhere,
        scratch_shapes=[
            pltpu.VMEM((half, cells, chans), BF16),
            pltpu.VMEM((half, cells, chans), BF16),
            pltpu.VMEM((half, cells, chans), BF16),
            pltpu.VMEM((2 * half, cells, inner), BF16),
            pltpu.VMEM((2 * half, 2, cols, inner), BF16),
            pltpu.VMEM((2, chans, inner), BF16),
            pltpu.VMEM((2, 9 * inner, inner), BF16),
            pltpu.VMEM((2, inner, chans), BF16),
            pltpu.VMEM((2, 8, chans), F32),
            dma((half,)), dma((4,)), dma((half, 2)), dma((half, 2)), dma((half,)), dma((half,)), dma((half,)),
            dma((2 * half, 2)), dma((2 * half, 2)), dma((4,)), dma((4,)), dma((3, 3)), dma((3, 3)),
        ],
        compiler_params=pltpu.CompilerParams(
            collective_id=0, has_side_effects=True, vmem_limit_bytes=56 * 1024 * 1024
        ),
    )(
        features.reshape(slides, cells, chans),
        mask,
        w_reduce[0],
        w_spatial.reshape(9 * inner, inner),
        w_expand[0],
        bias,
    )
    return result.reshape(1, slides, rows, cols, chans)


def solution(mesh):
    in_specs = (
        P(None, "strip", None, None),
        P(None, "strip", None),
        P("section", None, None),
        P("section", None),
        P("section", None, None, None, None),
        P("section", None),
        P("section", None, None),
        P("section", None),
    )
    out_specs = P("section", None, "strip", None, None)
    body = functools.partial(shards, mesh.shape["strip"], mesh.shape["section"])
    return jax.shard_map(body, mesh=mesh, in_specs=in_specs, out_specs=out_specs, check_vma=False)
```

```python
import functools

import jax
import jax.numpy as jnp
from jax import lax
from jax.experimental import pallas as pl
from jax.experimental.pallas import tpu as pltpu
from jax.sharding import PartitionSpec as P

TILE_W = 8
F32 = jnp.float32
BF16 = jnp.bfloat16


def tissue_mask(tile_list, rows):
    tiles_count = tile_list.shape[-1]
    columns = jnp.arange(tiles_count, dtype=jnp.int32)
    hits = jnp.any(tile_list[..., :, None] == columns[None, None, None, :], axis=-2)
    tissue = hits.astype(jnp.float32)
    tissue = jnp.repeat(tissue, rows, axis=1)
    return jnp.repeat(tissue, TILE_W, axis=2)


def kernel(
    strips, sections, half, cols, chans, inner,
    feat, mask, w1, w2, w3, bias, out,
    inbuf, mid, fin, stage, halo, v1, v2, v3, vb,
    feat_sem, own_sem, in_sem, fwd_sem, loc_sem, out_send, out_recv,
    halo_send, halo_recv, w_send, w_recv, m_send, m_recv,
):
    p = lax.axis_index("strip")
    s = lax.axis_index("section")
    pair = s // 2
    b = s % 2
    c = p % 2
    q = p % 4
    side = q // 2
    pairs = sections // 2
    partner = {"section": s + 1 - 2 * b}
    mate = {"strip": p + 1 - 2 * c}
    across = {"strip": p + 2 - 4 * side}
    up, down = {"strip": p - 1}, {"strip": p + 1}
    ahead, behind = {"section": s + 2}, {"section": s - 2}
    has_up, has_down = p > 0, p < strips - 1
    first, last = pair == 0, pair == pairs - 1
    MESH = pl.DeviceIdType.MESH

    def remote(src, dst, send, recv, to):
        return pltpu.make_async_remote_copy(
            src_ref=src, dst_ref=dst, send_sem=send, recv_sem=recv, device_id=to, device_id_type=MESH
        )

    barrier = pltpu.get_barrier_semaphore()

    def greet(to):
        pl.semaphore_signal(barrier, inc=1, device_id=to, device_id_type=MESH)

    greet(partner)
    greet(across)
    pl.when(has_up)(lambda: greet(up))
    pl.when(has_down)(lambda: greet(down))
    pl.when(jnp.logical_not(last))(lambda: greet(ahead))
    pl.when(jnp.logical_not(first))(lambda: greet(behind))

    weights = ((w1, v1), (w2, v2), (w3, v3))

    def own_copies():
        made = [pltpu.make_async_copy(w, v.at[b], own_sem.at[i]) for i, (w, v) in enumerate(weights)]
        return made + [pltpu.make_async_copy(bias, vb.at[b], own_sem.at[3])]

    def feat_copy(j):
        return pltpu.make_async_copy(feat.at[b * half + j], inbuf.at[j], feat_sem.at[j])

    for one in own_copies():
        one.start()

    @pl.when(first)
    def _():
        for j in range(half):
            feat_copy(j).start()

    def zero_edge(edge):
        def body(t, carry):
            halo[t, edge] = jnp.zeros((cols, inner), BF16)
            return carry

        lax.fori_loop(0, 2 * half, body, 0)

    pl.when(jnp.logical_not(has_up))(lambda: zero_edge(0))
    pl.when(jnp.logical_not(has_down))(lambda: zero_edge(1))

    peers = 2 + sum(jnp.where(met, 1, 0) for met in (has_up, has_down, pair < pairs - 1, pair > 0))
    pl.semaphore_wait(barrier, peers)

    def quarter(i, which):
        depth = weights[i][0].shape[0] // 4
        return pl.ds(pl.multiple_of(which * depth, depth), depth)

    def part_copy(i):
        if i == 3:
            return remote(bias, vb.at[b], w_send.at[3], w_recv.at[3], partner)
        w, v = weights[i]
        rows = quarter(i, q)
        return remote(w.at[rows], v.at[b, rows], w_send.at[i], w_recv.at[i], partner)

    def spread(i, which, slot, to):
        where = weights[i][1].at[1 - b, quarter(i, which)]
        return remote(where, where, m_send.at[slot, i], m_recv.at[slot, i], to)

    def mate_copy(i):
        return spread(i, q, 0, mate)

    def across_copy(i):
        return spread(i, q, 1, across)

    def onward_copy(i):
        return spread(i, (q + 2) % 4, 2, mate)

    for i in (3, 0, 1, 2):
        part_copy(i).start()

    def wait_own():
        for one in own_copies():
            one.wait()

    def wait_other():
        part_copy(3).wait_recv()
        part_copy(0).wait_recv()
        across_copy(0).start()
        mate_copy(0).start()
        for i in range(3):
            if i < 2:
                part_copy(i + 1).wait_recv()
                across_copy(i + 1).start()
                mate_copy(i + 1).start()
            across_copy(i).wait_recv()
            onward_copy(i).start()
        for i in range(3):
            mate_copy(i).wait_recv()
            onward_copy(i).wait_recv()

    def halo_up(t):
        return remote(
            stage.at[t, pl.ds(0, cols)], halo.at[t, 1], halo_send.at[t, 0], halo_recv.at[t, 1], up
        )

    def halo_down(t):
        return remote(
            stage.at[t, pl.ds(cols, cols)], halo.at[t, 0], halo_send.at[t, 1], halo_recv.at[t, 0], down
        )

    column = lax.broadcasted_iota(jnp.int32, (2 * cols, inner), 0) % cols

    def dot(lhs, rhs):
        return jnp.dot(lhs, rhs, preferred_element_type=F32)

    def block(which, j, src, dst):
        t = which * half + j
        reduced = dot(src[j], v1[which]) + vb[which, 0:1, 0:inner]
        stage[t] = jnp.maximum(reduced, 0.0).astype(BF16)
        pl.when(has_up)(lambda: halo_up(t).start())
        pl.when(has_down)(lambda: halo_down(t).start())

        def tap(dy, dx):
            return v2[which, pl.ds((dy * 3 + dx) * inner, inner), :]

        both = stage[t]
        upper, lower = both[:cols], both[cols:]
        sums = []
        for dx in range(3):
            centre = dot(both, tap(1, dx))
            cross = jnp.concatenate([dot(lower, tap(2, dx)), dot(upper, tap(0, dx))], axis=0)
            sums.append(centre + cross)
        pl.when(has_up)(lambda: halo_down(t).wait_recv())
        pl.when(has_down)(lambda: halo_up(t).wait_recv())
        above, below = halo[t, 0], halo[t, 1]
        for dx in range(3):
            sums[dx] += jnp.concatenate([dot(above, tap(0, dx)), dot(below, tap(2, dx))], axis=0)
        left = jnp.where(column == 0, 0.0, pltpu.roll(sums[0], 1, 0))
        right = jnp.where(column == cols - 1, 0.0, pltpu.roll(sums[2], 2 * cols - 1, 0))
        total = sums[1] + left + right + vb[which, 1:2, 0:inner]
        spatial = jnp.maximum(total, 0.0).astype(BF16)
        kept = mask[b * half + j][:, 0:1]
        for low in range(0, chans, inner):
            span = pl.ds(low, inner)
            value = src[j, :, span].astype(F32) + dot(spatial, v3[which, :, span]) + vb[which, 2:3, span]
            dst[j, :, span] = (jnp.maximum(value, 0.0) * kept).astype(BF16)

    def in_copy(j):
        return remote(fin.at[j], inbuf.at[j], fwd_sem.at[j], in_sem.at[j], ahead)

    def out_local(buffer, j):
        return pltpu.make_async_copy(buffer.at[j], out.at[b * half + j], loc_sem.at[j])

    def out_remote(buffer, j):
        return remote(buffer.at[j], out.at[b * half + j], out_send.at[j], out_recv.at[j], partner)

    pl.when(b == 0)(wait_own)
    pl.when(b == 1)(wait_other)

    def one_slide(j, carry):
        pl.when(first)(lambda: feat_copy(j).wait())
        pl.when(jnp.logical_not(first))(lambda: in_copy(j).wait_recv())
        block(0, j, inbuf, mid)
        pl.when(b == 0)(lambda: out_local(mid, j).start())
        pl.when(b == 1)(lambda: out_remote(mid, j).start())

        @pl.when(j == 0)
        def _():
            pl.when(b == 0)(wait_other)
            pl.when(b == 1)(wait_own)

        block(1, j, mid, fin)

        @pl.when(jnp.logical_not(last))
        def _():
            pl.when(j > 0)(lambda: in_copy(j - 1).wait_send())
            in_copy(j).start()

        pl.when(b == 1)(lambda: out_local(fin, j).start())
        pl.when(b == 0)(lambda: out_remote(fin, j).start())
        return carry

    lax.fori_loop(0, half, one_slide, 0)

    part_copy(3).wait_send()
    for i in range(3):
        part_copy(i).wait_send()
        mate_copy(i).wait_send()
        across_copy(i).wait_send()
        onward_copy(i).wait_send()

    def drain(j, carry):
        for t in (j, half + j):
            pl.when(has_up)(lambda t=t: halo_up(t).wait_send())
            pl.when(has_down)(lambda t=t: halo_down(t).wait_send())
        out_local(mid, j).wait()
        out_remote(mid, j).wait()
        return carry

    lax.fori_loop(0, half, drain, 0)
    pl.when(jnp.logical_not(last))(lambda: in_copy(half - 1).wait_send())


def shards(
    strips, sections,
    features, tile_list, w_reduce, bias_reduce, w_spatial, bias_spatial, w_expand, bias_expand,
):
    slides, rows, cols, chans = features.shape
    inner = w_reduce.shape[-1]
    half = slides // 2
    cells = rows * cols
    tissue = tissue_mask(tile_list, rows).reshape(slides, cells, 1)
    mask = jnp.broadcast_to(tissue, (slides, cells, 128))
    bias = jnp.zeros((8, chans), F32)
    bias = bias.at[0, :inner].set(bias_reduce[0].astype(F32))
    bias = bias.at[1, :inner].set(bias_spatial[0].astype(F32))
    bias = bias.at[2].set(bias_expand[0].astype(F32))
    dma = pltpu.SemaphoreType.DMA
    anywhere = pl.BlockSpec(memory_space=pl.ANY)
    result = pl.pallas_call(
        functools.partial(kernel, strips, sections, half, cols, chans, inner),
        out_shape=jax.ShapeDtypeStruct((slides, cells, chans), BF16),
        in_specs=[anywhere, pl.BlockSpec(memory_space=pltpu.VMEM)] + [anywhere] * 4,
        out_specs=anywhere,
        scratch_shapes=[
            pltpu.VMEM((half, cells, chans), BF16),
            pltpu.VMEM((half, cells, chans), BF16),
            pltpu.VMEM((half, cells, chans), BF16),
            pltpu.VMEM((2 * half, cells, inner), BF16),
            pltpu.VMEM((2 * half, 2, cols, inner), BF16),
            pltpu.VMEM((2, chans, inner), BF16),
            pltpu.VMEM((2, 9 * inner, inner), BF16),
            pltpu.VMEM((2, inner, chans), BF16),
            pltpu.VMEM((2, 8, chans), F32),
            dma((half,)), dma((4,)), dma((half,)), dma((half,)), dma((half,)), dma((half,)), dma((half,)),
            dma((2 * half, 2)), dma((2 * half, 2)), dma((4,)), dma((4,)), dma((3, 3)), dma((3, 3)),
        ],
        compiler_params=pltpu.CompilerParams(
            collective_id=0, has_side_effects=True, vmem_limit_bytes=40 * 1024 * 1024
        ),
    )(
        features.reshape(slides, cells, chans),
        mask,
        w_reduce[0],
        w_spatial.reshape(9 * inner, inner),
        w_expand[0],
        bias,
    )
    return result.reshape(1, slides, rows, cols, chans)


def solution(mesh):
    in_specs = (
        P(None, "strip", None, None),
        P(None, "strip", None),
        P("section", None, None),
        P("section", None),
        P("section", None, None, None, None),
        P("section", None),
        P("section", None, None),
        P("section", None),
    )
    out_specs = P("section", None, "strip", None, None)
    body = functools.partial(shards, mesh.shape["strip"], mesh.shape["section"])
    return jax.shard_map(body, mesh=mesh, in_specs=in_specs, out_specs=out_specs, check_vma=False)
```

```python
import functools

import jax
import jax.numpy as jnp
from jax import lax
from jax.experimental import pallas as pl
from jax.experimental.pallas import tpu as pltpu
from jax.sharding import PartitionSpec as P

TILE_W = 8
F32 = jnp.float32
BF16 = jnp.bfloat16


def tissue_mask(tile_list, rows):
    tiles_count = tile_list.shape[-1]
    columns = jnp.arange(tiles_count, dtype=jnp.int32)
    hits = jnp.any(tile_list[..., :, None] == columns[None, None, None, :], axis=-2)
    tissue = hits.astype(jnp.float32)
    tissue = jnp.repeat(tissue, rows, axis=1)
    return jnp.repeat(tissue, TILE_W, axis=2)


def kernel(
    strips, sections, half, cols, chans, inner,
    feat, mask, w1, w2, w3, bias, out,
    inbuf, mid, fin, stage, halo, v1, v2, v3, vb,
    feat_sem, own_sem, in_sem, fwd_sem, loc_sem, out_send, out_recv,
    halo_send, halo_recv, w_send, w_recv, m_send, m_recv,
):
    p = lax.axis_index("strip")
    s = lax.axis_index("section")
    pair = s // 2
    b = s % 2
    c = p % 2
    pairs = sections // 2
    partner = {"section": s + 1 - 2 * b}
    mate = {"strip": p + 1 - 2 * c}
    up, down = {"strip": p - 1}, {"strip": p + 1}
    ahead, behind = {"section": s + 2}, {"section": s - 2}
    has_up, has_down = p > 0, p < strips - 1
    first, last = pair == 0, pair == pairs - 1
    MESH = pl.DeviceIdType.MESH

    def remote(src, dst, send, recv, to):
        return pltpu.make_async_remote_copy(
            src_ref=src, dst_ref=dst, send_sem=send, recv_sem=recv, device_id=to, device_id_type=MESH
        )

    barrier = pltpu.get_barrier_semaphore()

    def greet(to):
        pl.semaphore_signal(barrier, inc=1, device_id=to, device_id_type=MESH)

    greet(partner)
    pl.when(has_up)(lambda: greet(up))
    pl.when(has_down)(lambda: greet(down))
    pl.when(jnp.logical_not(last))(lambda: greet(ahead))
    pl.when(jnp.logical_not(first))(lambda: greet(behind))

    weights = ((w1, v1), (w2, v2), (w3, v3))

    def own_copies():
        made = [pltpu.make_async_copy(w, v.at[b], own_sem.at[i]) for i, (w, v) in enumerate(weights)]
        return made + [pltpu.make_async_copy(bias, vb.at[b], own_sem.at[3])]

    def feat_copy(j):
        return pltpu.make_async_copy(feat.at[b * half + j], inbuf.at[j], feat_sem.at[j])

    for one in own_copies():
        one.start()

    @pl.when(first)
    def _():
        for j in range(half):
            feat_copy(j).start()

    def zero_edge(side):
        def body(t, carry):
            halo[t, side] = jnp.zeros((cols, inner), BF16)
            return carry

        lax.fori_loop(0, 2 * half, body, 0)

    pl.when(jnp.logical_not(has_up))(lambda: zero_edge(0))
    pl.when(jnp.logical_not(has_down))(lambda: zero_edge(1))

    peers = 1 + sum(jnp.where(met, 1, 0) for met in (has_up, has_down, pair < pairs - 1, pair > 0))
    pl.semaphore_wait(barrier, peers)

    def part_copies():
        made = []
        for i, (w, v) in enumerate(weights):
            depth = w.shape[0] // 2
            rows = pl.ds(pl.multiple_of(c * depth, depth), depth)
            made.append(remote(w.at[rows], v.at[b, rows], w_send.at[i], w_recv.at[i], partner))
        made.append(remote(bias, vb.at[b], w_send.at[3], w_recv.at[3], partner))
        return made

    def mate_copies():
        made = []
        for i, (w, v) in enumerate(weights):
            depth = w.shape[0] // 2
            rows = pl.ds(pl.multiple_of(c * depth, depth), depth)
            where = v.at[1 - b, rows]
            made.append(remote(where, where, m_send.at[i], m_recv.at[i], mate))
        return made

    for i in (3, 0, 1, 2):
        part_copies()[i].start()

    def wait_own():
        for one in own_copies():
            one.wait()

    def wait_other():
        part_copies()[3].wait_recv()
        for i in range(3):
            part_copies()[i].wait_recv()
            mate_copies()[i].start()
        for i in range(3):
            mate_copies()[i].wait_recv()

    def halo_up(t):
        return remote(
            stage.at[t, pl.ds(0, cols)], halo.at[t, 1], halo_send.at[t, 0], halo_recv.at[t, 1], up
        )

    def halo_down(t):
        return remote(
            stage.at[t, pl.ds(cols, cols)], halo.at[t, 0], halo_send.at[t, 1], halo_recv.at[t, 0], down
        )

    column = lax.broadcasted_iota(jnp.int32, (2 * cols, inner), 0) % cols

    def dot(lhs, rhs):
        return jnp.dot(lhs, rhs, preferred_element_type=F32)

    def block(which, j, src, dst, arrived, finished):
        t = which * half + j
        for r in range(2):
            arrived(r)
            reduced = dot(src[j, pl.ds(r * cols, cols)], v1[which]) + vb[which, 0:1, 0:inner]
            stage[t, pl.ds(r * cols, cols)] = jnp.maximum(reduced, 0.0).astype(BF16)
            if r == 0:
                pl.when(has_up)(lambda: halo_up(t).start())
            else:
                pl.when(has_down)(lambda: halo_down(t).start())

        def tap(dy, dx):
            return v2[which, pl.ds((dy * 3 + dx) * inner, inner), :]

        both = stage[t]
        upper, lower = both[:cols], both[cols:]
        sums = []
        for dx in range(3):
            centre = dot(both, tap(1, dx))
            cross = jnp.concatenate([dot(lower, tap(2, dx)), dot(upper, tap(0, dx))], axis=0)
            sums.append(centre + cross)
        pl.when(has_up)(lambda: halo_down(t).wait_recv())
        pl.when(has_down)(lambda: halo_up(t).wait_recv())
        above, below = halo[t, 0], halo[t, 1]
        for dx in range(3):
            sums[dx] += jnp.concatenate([dot(above, tap(0, dx)), dot(below, tap(2, dx))], axis=0)
        left = jnp.where(column == 0, 0.0, pltpu.roll(sums[0], 1, 0))
        right = jnp.where(column == cols - 1, 0.0, pltpu.roll(sums[2], 2 * cols - 1, 0))
        total = sums[1] + left + right + vb[which, 1:2, 0:inner]
        spatial = jnp.maximum(total, 0.0).astype(BF16)
        for r in range(2):
            part = pl.ds(r * cols, cols)
            kept = mask[b * half + j, part, 0:1]
            for low in range(0, chans, inner):
                span = pl.ds(low, inner)
                value = dot(spatial[r * cols : (r + 1) * cols], v3[which, :, span])
                value += src[j, part, span].astype(F32) + vb[which, 2:3, span]
                dst[j, part, span] = (jnp.maximum(value, 0.0) * kept).astype(BF16)
            finished(r)

    def in_copy(j, r):
        part = pl.ds(r * cols, cols)
        return remote(
            fin.at[j, part], inbuf.at[j, part], fwd_sem.at[j, r], in_sem.at[j, r], ahead
        )

    def out_local(buffer, j):
        return pltpu.make_async_copy(buffer.at[j], out.at[b * half + j], loc_sem.at[j])

    def out_remote(buffer, j):
        return remote(buffer.at[j], out.at[b * half + j], out_send.at[j], out_recv.at[j], partner)

    pl.when(b == 0)(wait_own)
    pl.when(b == 1)(wait_other)

    def one_slide(j, carry):
        pl.when(first)(lambda: feat_copy(j).wait())

        def arrived(r):
            pl.when(jnp.logical_not(first))(lambda: in_copy(j, r).wait_recv())

        def finished(r):
            pl.when(jnp.logical_not(last))(lambda: in_copy(j, r).start())

        def nothing(r):
            pass

        block(0, j, inbuf, mid, arrived, nothing)
        pl.when(b == 0)(lambda: out_local(mid, j).start())
        pl.when(b == 1)(lambda: out_remote(mid, j).start())

        @pl.when(j == 0)
        def _():
            pl.when(b == 0)(wait_other)
            pl.when(b == 1)(wait_own)

        block(1, j, mid, fin, nothing, finished)
        pl.when(b == 1)(lambda: out_local(fin, j).start())
        pl.when(b == 0)(lambda: out_remote(fin, j).start())
        return carry

    lax.fori_loop(0, half, one_slide, 0)

    for one in part_copies() + mate_copies():
        one.wait_send()

    def drain(j, carry):
        for t in (j, half + j):
            pl.when(has_up)(lambda t=t: halo_up(t).wait_send())
            pl.when(has_down)(lambda t=t: halo_down(t).wait_send())
        for r in range(2):
            pl.when(jnp.logical_not(last))(lambda r=r: in_copy(j, r).wait_send())
        out_local(mid, j).wait()
        out_remote(mid, j).wait()
        return carry

    lax.fori_loop(0, half, drain, 0)


def shards(
    strips, sections,
    features, tile_list, w_reduce, bias_reduce, w_spatial, bias_spatial, w_expand, bias_expand,
):
    slides, rows, cols, chans = features.shape
    inner = w_reduce.shape[-1]
    half = slides // 2
    cells = rows * cols
    tissue = tissue_mask(tile_list, rows).reshape(slides, cells, 1)
    mask = jnp.broadcast_to(tissue, (slides, cells, 128))
    bias = jnp.zeros((8, chans), F32)
    bias = bias.at[0, :inner].set(bias_reduce[0].astype(F32))
    bias = bias.at[1, :inner].set(bias_spatial[0].astype(F32))
    bias = bias.at[2].set(bias_expand[0].astype(F32))
    dma = pltpu.SemaphoreType.DMA
    anywhere = pl.BlockSpec(memory_space=pl.ANY)
    result = pl.pallas_call(
        functools.partial(kernel, strips, sections, half, cols, chans, inner),
        out_shape=jax.ShapeDtypeStruct((slides, cells, chans), BF16),
        in_specs=[anywhere, pl.BlockSpec(memory_space=pltpu.VMEM)] + [anywhere] * 4,
        out_specs=anywhere,
        scratch_shapes=[
            pltpu.VMEM((half, cells, chans), BF16),
            pltpu.VMEM((half, cells, chans), BF16),
            pltpu.VMEM((half, cells, chans), BF16),
            pltpu.VMEM((2 * half, cells, inner), BF16),
            pltpu.VMEM((2 * half, 2, cols, inner), BF16),
            pltpu.VMEM((2, chans, inner), BF16),
            pltpu.VMEM((2, 9 * inner, inner), BF16),
            pltpu.VMEM((2, inner, chans), BF16),
            pltpu.VMEM((2, 8, chans), F32),
            dma((half,)), dma((4,)), dma((half, 2)), dma((half, 2)), dma((half,)), dma((half,)), dma((half,)),
            dma((2 * half, 2)), dma((2 * half, 2)), dma((4,)), dma((4,)), dma((3,)), dma((3,)),
        ],
        compiler_params=pltpu.CompilerParams(
            collective_id=0, has_side_effects=True, vmem_limit_bytes=56 * 1024 * 1024
        ),
    )(
        features.reshape(slides, cells, chans),
        mask,
        w_reduce[0],
        w_spatial.reshape(9 * inner, inner),
        w_expand[0],
        bias,
    )
    return result.reshape(1, slides, rows, cols, chans)


def solution(mesh):
    in_specs = (
        P(None, "strip", None, None),
        P(None, "strip", None),
        P("section", None, None),
        P("section", None),
        P("section", None, None, None, None),
        P("section", None),
        P("section", None, None),
        P("section", None),
    )
    out_specs = P("section", None, "strip", None, None)
    body = functools.partial(shards, mesh.shape["strip"], mesh.shape["section"])
    return jax.shard_map(body, mesh=mesh, in_specs=in_specs, out_specs=out_specs, check_vma=False)
```
